32 devices in a mesh: sub: 2 (over x), row: 4 (over y, core), col: 4 (over z).
Axes of the slice: x: 2, y: 2, z: 4, core: 2. Of those that a mesh axis runs over, the one named last changes fastest.
Arguments:
- front_panel: bfloat16 [16384, 3072], P(('sub', 'row', 'col')), may hold values from -6 to 6
- tile_inverse: bfloat16 [12, 256, 256], replicated
- front_trailing: float32 [16384, 16384], P(('sub', 'row'), 'col'), may hold values from -6 to 6
- child_update: bfloat16 [2, 5120, 5120], P('sub', 'col', 'row'), may hold values from -6 to 6
- child_map: int32 [2, 20], replicated, may hold values from 0 to 63, as said below
- pattern: int32 [64, 64], replicated, may hold values from 0 to 1, as said below
Outputs:
- factor: bfloat16 [16384, 3072], P(('sub', 'row', 'col'))
- trailing: float32 [16384, 16384], P(('sub', 'row'), 'col')
The draws below stay inside these ranges and needn't reach their ends.
Inputs may be any that keep to these rules, and one draw needn't show every extreme that they name: `child_map`: each row lists 20 distinct parent tiles in increasing order; the first child's row always holds tile 0 and tile 64 - 1. `pattern`: symmetric, with ones on the diagonal.
All inputs are finite; a program needn't handle non-finite values.
Results may differ from the reference program's by a relative error of at most 0.001.
Values may be sent and summed in bfloat16 or wider, within the bound.
No kernel may reach another device: no remote copies, remote signals or barrier semaphores. Data moves between devices by JAX's collectives and lax.ppermute only.
A program may use at most 320 MiB of HBM per device.

```python
import jax
import jax.numpy as jnp
from jax import lax

TILE = 256
NP = 3072
NU = 16384
NC = 5120
NPT = 12
NUT = 64
NCT = 20


def draw_tile_inverse(key, part):
    key_diag, key_off = jax.random.split(key)
    positions = jnp.arange(TILE)
    upper = (positions[:, None] < positions[None, :]).astype(jnp.float32)
    identity = jnp.eye(TILE, dtype=jnp.float32)
    diagonal = jnp.exp(jax.random.uniform(key_diag, (NPT, TILE), jnp.float32, jnp.log(0.02), jnp.log(0.06)))
    offdiag = 0.003 * jax.random.normal(key_off, (NPT, TILE, TILE), jnp.float32)
    return (diagonal[:, :, None] * identity[None, :, :] + offdiag * upper[None, :, :]).astype(jnp.bfloat16)


def draw_child_map(key, part):
    key_first, key_second = jax.random.split(jax.random.fold_in(key, 11))
    interior = jax.random.permutation(key_first, NUT - 2)[:NCT - 2].astype(jnp.int32) + 1
    first_map = jnp.sort(jnp.concatenate([jnp.zeros((1,), jnp.int32), interior, jnp.full((1,), NUT - 1, jnp.int32)]))
    second_map = jnp.sort(jax.random.permutation(key_second, NUT)[:NCT].astype(jnp.int32))
    return jnp.stack([first_map, second_map]).astype(jnp.int32)


def draw_pattern(key, part):
    key_bits, key_extra = jax.random.split(jax.random.fold_in(key, 23))
    positions = jnp.arange(NUT, dtype=jnp.int32)
    distance = jnp.abs(positions[:, None] - positions[None, :])
    extra_rows = jax.random.randint(key_extra, (NUT,), 0, 6)
    threshold = jnp.clip(10 - distance // 2 + extra_rows[:, None] + extra_rows[None, :], 1, 16)
    random_bits = jax.random.randint(key_bits, (NUT, NUT), 0, 16)
    below_diag = (random_bits < threshold) & (positions[:, None] > positions[None, :])
    chosen = below_diag | below_diag.T | (distance == 0)
    return chosen.astype(jnp.int32)


def block_scale(key, dims, cuts, smallest, top_value):
    loudness = 1.0
    for axis_at, parts in cuts:
        heights = jax.random.uniform(jax.random.fold_in(jax.random.fold_in(key, 6), axis_at), (parts,), jnp.float32, smallest / len(cuts), top_value / len(cuts))
        loudness = loudness * jnp.repeat(jnp.exp(heights), dims[axis_at] // parts).reshape((-1,) + (1,) * (len(dims) - 1 - axis_at))
    return loudness


def scatter_about(stream_key, extent, deviation, most, shards=(), held_as=jnp.bfloat16):
    drawn = deviation * jax.random.normal(stream_key, extent, jnp.float32)
    if shards:
        drawn = drawn * block_scale(stream_key, extent, shards, -0.22, 0.18)
    return jnp.clip(drawn, -most, most).astype(held_as)


def setup_inputs(seed: int = 0) -> dict:
    splits = jax.random.split(jax.random.key(seed), 7)
    front_panel = scatter_about(splits[0], (NU, NP), 1.0, 6.0, ((0, 32),))
    tile_inverse = draw_tile_inverse(jax.random.fold_in(splits[6], 71), 0)
    front_trailing = scatter_about(splits[2], (NU, NU), 1.0, 6.0, ((0, 8), (1, 4)), jnp.float32)
    child_update = scatter_about(splits[3], (2, NC, NC), 1.0, 6.0, ((0, 2), (1, 4), (2, 4)))
    child_map = draw_child_map(jax.random.fold_in(splits[6], 71), 0)
    pattern = draw_pattern(jax.random.fold_in(splits[6], 71), 0)
    return dict(front_panel=front_panel, tile_inverse=tile_inverse, front_trailing=front_trailing, child_update=child_update, child_map=child_map, pattern=pattern)


def apply_inverse(panel_rows, inverses):
    row_count = panel_rows.shape[0]
    tile_count = inverses.shape[0]
    tile_size = inverses.shape[1]
    shaped = panel_rows.astype(jnp.float32).reshape(row_count, tile_count, tile_size)
    scaled = jnp.einsum("rkt,kts->rks", shaped, inverses.astype(jnp.float32))
    return scaled.astype(jnp.bfloat16).reshape(row_count, tile_count * tile_size)


def reference(front_panel, tile_inverse, front_trailing, child_update, child_map, pattern):
    factor = apply_inverse(front_panel, tile_inverse)
    parents = jnp.arange(NUT, dtype=jnp.int32)
    spread = []
    for child_index in range(2):
        onehot = (child_map[child_index][:, None] == parents[None, :]).astype(jnp.float32)
        child_block = child_update[child_index].astype(jnp.float32).reshape(NCT, TILE, NCT, TILE)
        placed = jnp.einsum("iajb,jq->iaqb", child_block, onehot)
        spread.append(placed.reshape(NCT, TILE, NU))

    def one_row(tile_index):
        tile_rows = lax.dynamic_slice_in_dim(factor, tile_index * TILE, TILE, 0)
        product = lax.dot_general(tile_rows, factor, (((1,), (1,)), ((), ())), preferred_element_type=jnp.float32)
        mask_row = lax.dynamic_index_in_dim(pattern, tile_index, 0, keepdims=False).astype(jnp.float32)
        weights = jnp.repeat(mask_row, TILE)
        first_pick = (child_map[0] == tile_index).astype(jnp.float32)
        second_pick = (child_map[1] == tile_index).astype(jnp.float32)
        extend = jnp.einsum("i,iax->ax", first_pick, spread[0]) + jnp.einsum("i,iax->ax", second_pick, spread[1])
        base_rows = lax.dynamic_slice_in_dim(front_trailing, tile_index * TILE, TILE, 0)
        return (base_rows + extend) - product * weights[None, :]

    trailing = lax.map(one_row, jnp.arange(NUT, dtype=jnp.int32)).reshape(NU, NU)
    return factor, trailing
```

```python
import functools
import itertools

import jax
import jax.numpy as jnp
from jax import lax
from jax.experimental import pallas as pl
from jax.experimental.pallas import tpu as pltpu
from jax.sharding import PartitionSpec as P

COL_WINDOW = 8
ROW_WINDOWS = (14, 8, 6)
CHUNKS = 6
VMEM = 56 * 1024 * 1024


def spread(value, axis, source):
    kept = jnp.where(lax.axis_index(axis) == source, value, 0).astype(value.dtype)
    return lax.psum(kept, axis)


def partner(value, axis, distance):
    mask = 2**distance
    pairs = [(source, source ^ mask) for source in range(lax.axis_size(axis))]
    return lax.ppermute(value, axis, pairs)


def apply_inverse(panel_rows, inverses):
    row_count = panel_rows.shape[0]
    tile_count = inverses.shape[0]
    tile_size = inverses.shape[1]
    shaped = panel_rows.reshape(row_count, tile_count, tile_size)
    scaled = jnp.einsum("rkt,kts->rks", shaped, inverses, preferred_element_type=jnp.float32)
    return scaled.astype(jnp.bfloat16).reshape(row_count, tile_count * tile_size)


def place_columns(child_block, tile_map, parent_tiles, tile_size):
    row_count = child_block.shape[0]
    tile_count = tile_map.shape[0]
    wanted = jnp.arange(parent_tiles, dtype=jnp.int32)
    onehot = (tile_map[:, None] == wanted[None, :]).astype(jnp.bfloat16)
    placed = jnp.einsum(
        "rjt,jq->rqt",
        child_block.reshape(row_count, tile_count, tile_size),
        onehot,
        preferred_element_type=jnp.float32,
    )
    return placed.astype(jnp.bfloat16).reshape(row_count, parent_tiles * tile_size)


def pick_rows(child_block, tile_map, grid_block, tile_rows, tile_size):
    tile_count = tile_map.shape[0]
    width_cols = child_block.shape[1]
    wanted = grid_block * tile_rows + jnp.arange(tile_rows, dtype=jnp.int32)
    onehot = (tile_map[:, None] == wanted[None, :]).astype(jnp.bfloat16)
    picked = jnp.einsum(
        "itx,ip->ptx",
        child_block.reshape(tile_count, tile_size, width_cols),
        onehot,
        preferred_element_type=jnp.float32,
    )
    return picked.reshape(tile_rows * tile_size, width_cols)


def general_device(front_panel, tile_inverse, front_trailing, child_update, child_map, pattern):
    tile_size = tile_inverse.shape[1]
    parent_tiles = pattern.shape[0]
    block_rows = front_trailing.shape[0]
    block_cols = front_trailing.shape[1]
    tile_rows = block_rows // tile_size
    tile_cols = block_cols // tile_size
    sub_index = lax.axis_index("sub")
    row_index = lax.axis_index("row")
    col_index = lax.axis_index("col")
    rows_count = lax.axis_size("row")
    grid_row = sub_index * rows_count + row_index
    factor = apply_inverse(front_panel, tile_inverse)
    row_panel = lax.all_gather(factor, "col", axis=0, tiled=True)
    share_rows = min(block_rows, block_cols)
    pieces = []
    for part_index in range(block_cols // share_rows):
        first_row = col_index * block_cols + part_index * share_rows
        source = first_row // block_rows
        offset = first_row % block_rows
        share_block = lax.dynamic_slice_in_dim(row_panel, offset, share_rows, 0)
        pieces.append(spread(share_block, ("sub", "row"), source))
    column_panel = pieces[0] if len(pieces) == 1 else jnp.concatenate(pieces, axis=0)
    own_map = lax.dynamic_index_in_dim(child_map, sub_index, 0, keepdims=False)
    own_child = child_update[0]
    gathered = lax.all_gather(own_child, "row", axis=1, tiled=True)
    placed = place_columns(gathered, own_map, parent_tiles, tile_size)
    child_rows = lax.all_to_all(placed, "col", split_axis=1, concat_axis=0, tiled=True)
    own_part = pick_rows(child_rows, own_map, grid_row, tile_rows, tile_size)
    other_block = (1 - sub_index) * rows_count + row_index
    sibling_part = pick_rows(child_rows, own_map, other_block, tile_rows, tile_size).astype(
        jnp.bfloat16
    )
    received = partner(sibling_part, "sub", 0)
    extend = own_part + received.astype(jnp.float32)
    local_mask = lax.dynamic_slice(
        pattern, (grid_row * tile_rows, col_index * tile_cols), (tile_rows, tile_cols)
    )
    product = lax.dot_general(
        row_panel, column_panel, (((1,), (1,)), ((), ())), preferred_element_type=jnp.float32
    )
    weights = local_mask.astype(jnp.float32)
    masked = (
        product.reshape(tile_rows, tile_size, tile_cols, tile_size) * weights[:, None, :, None]
    ).reshape(block_rows, block_cols)
    trailing = front_trailing + extend - masked
    return (factor, trailing)


def factor_kernel(panel_ref, inverse_ref, out_ref, *chunk_refs):
    count, size, _ = inverse_ref.shape
    per_chunk = count // len(chunk_refs)
    for k in range(count):
        here = (slice(None), pl.ds(k * size, size))
        scaled = jnp.dot(
            panel_ref[here], inverse_ref[k], preferred_element_type=jnp.float32
        ).astype(out_ref.dtype)
        out_ref[here] = scaled
        chunk_refs[k // per_chunk][:, pl.ds(k % per_chunk * size, size)] = scaled


def scale_panel(panel, inverses, chunks):
    rows, depth = panel.shape
    size = inverses.shape[1]
    step, wide = rows // 4, depth // chunks
    block = pl.BlockSpec((step, depth), lambda i: (i, 0))
    shape = jax.ShapeDtypeStruct
    return pl.pallas_call(
        factor_kernel,
        grid=(rows // step,),
        in_specs=[block, pl.BlockSpec(inverses.shape, lambda i: (0, 0, 0))],
        out_specs=[block] + [pl.BlockSpec((step, wide), lambda i: (i, 0))] * chunks,
        out_shape=[shape(panel.shape, panel.dtype)] + [shape((rows, wide), panel.dtype)] * chunks,
        compiler_params=pltpu.CompilerParams(vmem_limit_bytes=VMEM),
        cost_estimate=pl.CostEstimate(
            flops=2 * rows * depth * size, bytes_accessed=6 * panel.size, transcendentals=0
        ),
    )(panel, inverses)


def extend_kernel(tile, parts, groups, order, count, row_at, col_at, me, base_ref, *refs):
    strips, out_ref = refs[:-1], refs[-1]
    i = pl.program_id(0)
    part = tile // parts
    window = col_at.shape[1] // groups

    @pl.when((i == 0) | (i < count[0]))
    def _():
        out_ref[...] = base_ref[...]

    for kid, group in itertools.product(range(2), range(groups)):

        @pl.when((i < count[0]) & (row_at[kid * parts, order[i]] >= 0))
        def _():
            @pl.loop(0, window)
            def _(b):
                q = col_at[kid, group * window + b]

                @pl.when(q >= 0)
                def _():
                    lanes = pl.ds(pl.multiple_of(q * tile, tile), tile)
                    for m in range(parts):
                        strip_ref = strips[(group * 2 + kid) * parts + m]
                        first = pl.multiple_of((me[0] ^ m) * part, part)
                        here = (pl.ds(first, part), lanes)
                        out_ref[here] += strip_ref[0, b].astype(jnp.float32)


def extend_add(base, strips, tables, me, tile):
    height, width = base.shape
    parts = tile // strips[0].shape[2]
    groups = len(strips) // (2 * parts)
    order, count, row_at, col_at = tables

    def strip_spec(i):
        return pl.BlockSpec(
            (1,) + strips[i].shape[1:],
            lambda p, order, count, row_at, *_: (
                jnp.maximum(row_at[i % (2 * parts), order[p]], 0),
                0,
                0,
                0,
            ),
        )

    block = pl.BlockSpec((tile, width), lambda p, order, *_: (order[p], 0))
    return pl.pallas_call(
        functools.partial(extend_kernel, tile, parts, groups),
        grid_spec=pltpu.PrefetchScalarGridSpec(
            num_scalar_prefetch=5,
            grid=(height // tile,),
            in_specs=[block] + [strip_spec(i) for i in range(len(strips))],
            out_specs=block,
        ),
        out_shape=jax.ShapeDtypeStruct(base.shape, base.dtype),
        input_output_aliases={5: 0},
        compiler_params=pltpu.CompilerParams(vmem_limit_bytes=VMEM),
        cost_estimate=pl.CostEstimate(
            flops=base.size, bytes_accessed=4 * base.size, transcendentals=0
        ),
    )(order, count.reshape(1), row_at, col_at, me.reshape(1), base, *strips)


def update_kernel(tile, count, core, mask, *refs):
    rows, mine, other = (refs[k * count : (k + 1) * count] for k in range(3))
    base_ref, out_ref = refs[3 * count :]
    i, c = pl.program_id(0), pl.program_id(1)
    high, wide = out_ref.shape[0] // tile, out_ref.shape[1] // tile
    per_side = pl.num_programs(1) // 2
    first = column_block(c, per_side, core) * wide
    for side, cols in enumerate((mine, other)):

        @pl.when(c // per_side == side)
        def _():
            for q in range(wide):
                lanes = pl.ds(q * tile, tile)
                product = sum(
                    lax.dot_general(
                        rows_ref[...],
                        cols_ref[lanes, :],
                        (((1,), (1,)), ((), ())),
                        preferred_element_type=jnp.float32,
                    )
                    for rows_ref, cols_ref in zip(rows, cols)
                )
                for a in range(high):
                    here = (pl.ds(a * tile, tile), lanes)
                    reached = mask[i * high + a, first + q].astype(jnp.float32)
                    part = product[a * tile : (a + 1) * tile]
                    out_ref[here] = base_ref[here] - reached * part


def column_block(c, per_side, core):
    return (c // per_side ^ core[0]) * per_side + c % per_side


def update(base, rows, mine, other, mask, core, tile, in_place):
    height, width = base.shape
    step = 4 * tile
    per_side = width // step // 2
    block = pl.BlockSpec((step, step), lambda i, c, core, _: (i, column_block(c, per_side, core)))
    row_block = lambda i, c, *_: (i, 0)
    mine_block = lambda i, c, *_: (jnp.minimum(c, per_side - 1), 0)
    other_block = lambda i, c, *_: (jnp.maximum(c - per_side, 0), 0)
    specs = [
        pl.BlockSpec((step, piece.shape[1]), at)
        for pieces, at in ((rows, row_block), (mine, mine_block), (other, other_block))
        for piece in pieces
    ]
    depth = sum(piece.shape[1] for piece in rows)
    return pl.pallas_call(
        functools.partial(update_kernel, tile, len(rows)),
        grid_spec=pltpu.PrefetchScalarGridSpec(
            num_scalar_prefetch=2,
            grid=(height // step, width // step),
            in_specs=specs + [block],
            out_specs=block,
        ),
        out_shape=jax.ShapeDtypeStruct(base.shape, base.dtype),
        input_output_aliases={2 + 3 * len(rows): 0} if in_place else {},
        compiler_params=pltpu.CompilerParams(vmem_limit_bytes=VMEM),
        cost_estimate=pl.CostEstimate(
            flops=2 * height * width * depth, bytes_accessed=8 * base.size, transcendentals=0
        ),
    )(core.reshape(1), mask, *rows, *mine, *other, base)


def xor_permute(value, axes, size, mask):
    if mask == 0:
        return value
    return lax.ppermute(value, axes, [(i, i ^ mask) for i in range(size)])


def line_device(front_panel, tile_inverse, front_trailing, child_update, child_map, pattern):
    tile = tile_inverse.shape[1]
    block_rows, block_cols = front_trailing.shape
    tile_rows, tile_cols = block_rows // tile, block_cols // tile
    subs, rows, planes = (lax.axis_size(name) for name in ("sub", "row", "col"))
    grid = subs * rows
    cores = 2
    plane_axes = ("sub", "row")
    s, r, z = (lax.axis_index(name) for name in ("sub", "row", "col"))
    grid_row = s * rows + r
    chip, core = grid_row // cores, grid_row % cores
    shard = front_panel.shape[0]

    factor, *chunks = scale_panel(front_panel, tile_inverse, CHUNKS)

    child = child_update[0]
    own_rows, own_cols = child.shape[0] // tile, child.shape[1] // tile
    child_tiles = child_map.shape[1]
    part = tile // rows
    col_window = min(COL_WINDOW, child_tiles)
    row_windows = [min(size, child_tiles) for size in ROW_WINDOWS]

    def send_strips():
        shaped = child.reshape(own_rows, rows, part, own_cols, tile).transpose(1, 0, 3, 2, 4)
        return [
            xor_permute(
                lax.dynamic_index_in_dim(shaped, r ^ m, 0, keepdims=False), "row", rows, m
            )
            for m in range(rows)
        ]

    def edges_of(count):
        first = jnp.arange(count + 1, dtype=jnp.int32) * (pattern.shape[0] // count)
        return (child_map[:, None, :] < first[None, :, None]).sum(-1, dtype=jnp.int32)

    def rounds_of(edges, size):
        return (jnp.max(edges[:, 1:] - edges[:, :-1]) + size - 1) // size

    col_edges = edges_of(planes)
    row_edges = [edges_of(count) for count in (subs, subs * rows // cores, grid)]
    rounds = [rounds_of(col_edges, col_window)]
    rounds += [rounds_of(edges, size) for edges, size in zip(row_edges, row_windows)]

    def turns_of(turn):
        turns = []
        for count in reversed(rounds):
            turns.append(turn % count)
            turn = turn // count
        return turns[::-1]

    def col_start(kid, plane, turn):
        return jnp.minimum(col_edges[kid, plane] + turn * col_window, child_tiles - col_window)

    def row_starts(kid, row, turns):
        start, size, found = 0, child_tiles, []
        places_at = (row // rows, row // cores, row)
        for edges, at, turn, window in zip(row_edges, places_at, turns, row_windows):
            start = jnp.clip(edges[kid, at] + turn * window, start, start + size - window)
            size = window
            found.append(start)
        return found

    def send_columns(strips, turn):
        stripped = jnp.zeros((own_rows, child_tiles, part, tile), child.dtype)
        for m, got in enumerate(strips):
            stripped = lax.dynamic_update_slice(stripped, got, (0, (r ^ m) * own_cols, 0, 0))
        pieces = []
        for m in range(planes):
            start = col_start(s, z ^ m, turn)
            piece = lax.dynamic_slice_in_dim(stripped, start, col_window, 1)
            pieces.append(xor_permute(piece, "col", planes, m))
        return pieces

    def join_columns(pieces):
        groups = []
        for half in range(2):
            placed = jnp.zeros((child_tiles, col_window // 2, part, tile), child.dtype)
            for m, got in enumerate(pieces):
                got = got[:, half * col_window // 2 : (half + 1) * col_window // 2]
                placed = lax.dynamic_update_slice(placed, got, ((z ^ m) * own_rows, 0, 0, 0))
            groups.append(placed)
        return groups

    def taken(value, start, size):
        return lax.dynamic_slice_in_dim(value, start, size, 0)

    kids = (s, 1 - s)

    size = row_windows[1]

    def rows_for(values, row, turns, level=None):
        parts = []
        for value, kid in zip(values, kids):
            found = row_starts(kid, row, turns)
            first = 0 if level is None else found[level]
            parts.append(taken(value, found[1] - first, size))
        return parts

    def halves_first(placed, turns):
        here, there = (row_starts(s, row, turns)[0] for row in (grid_row, grid_row ^ rows))
        window = row_windows[0]
        return [
            taken(placed, here, window),
            xor_permute(taken(placed, there, window), "sub", subs, 1),
        ]

    def chips_second(halves, turns):
        here, there = (
            jnp.concatenate(rows_for(halves, row, turns, 0), axis=0)
            for row in (grid_row, grid_row ^ cores)
        )
        return [here, xor_permute(there, "row", rows, cores)]

    def chips_first(placed, turns):
        def of_both_halves(row):
            found = [rows_for([placed], half * rows + row, turns)[0] for half in range(subs)]
            return jnp.concatenate(found, axis=0)

        return [of_both_halves(r), xor_permute(of_both_halves(r ^ cores), "row", rows, cores)]

    def halves_second(strips, turns):
        here, there = (
            [taken(strip, half * size, size) for strip in strips] for half in kids
        )
        got = xor_permute(jnp.concatenate(there, axis=0), "sub", subs, 1)
        return [
            jnp.concatenate((kept, got[k * size : (k + 1) * size]), axis=0)
            for k, kept in enumerate(here)
        ]

    def send_cores(strips, turns):
        found = [row_starts(kid, grid_row ^ 1, turns) for kid in kids]
        parts = [
            taken(strip, kid * size + at[2] - at[1], row_windows[2])
            for strip in strips
            for kid, at in enumerate(found)
        ]
        return xor_permute(jnp.concatenate(parts, axis=0), "row", rows, 1)

    def tables_of(turns):
        col_turn, row_turns = turns[0], turns[1:]
        col_at, row_at = [], []
        wanted = grid_row * tile_rows + jnp.arange(tile_rows, dtype=jnp.int32)
        for place, kid in enumerate(kids):
            own_map = lax.dynamic_index_in_dim(child_map, kid, 0, keepdims=False)
            first = col_edges[kid, z] + col_turn * col_window
            last = jnp.minimum(first + col_window, col_edges[kid, z + 1])
            start = col_start(kid, z, col_turn)
            slot = start + jnp.arange(col_window, dtype=jnp.int32)
            parent = lax.dynamic_slice_in_dim(own_map, start, col_window) - z * tile_cols
            col_at.append(jnp.where((slot >= first) & (slot < last), parent, -1))

            same = own_map[None, :] == wanted[:, None]
            slot = jnp.max(jnp.where(same, jnp.arange(child_tiles, dtype=jnp.int32), -1), axis=1)
            held = slot >= 0
            at_level = (s, chip, grid_row)
            for edges, at, turn, window in zip(row_edges, at_level, row_turns, row_windows):
                first = edges[kid, at] + turn * window
                held &= (slot >= first) & (slot < first + window)
            starts = row_starts(kid, grid_row, row_turns)
            near_at = place * row_windows[1] + slot - starts[1]
            far_at = [(k * 2 + place) * row_windows[2] + slot - starts[2] for k in range(2)]
            order = (near_at, far_at[0], near_at, far_at[1])
            row_at += [jnp.where(held, at, -1) for at in order]
        row_at, col_at = jnp.stack(row_at), jnp.stack(col_at)
        reached = jnp.max(row_at, axis=0) >= 0
        count = jnp.sum(reached, dtype=jnp.int32)
        every = jnp.arange(tile_rows, dtype=jnp.int32)
        before = jnp.sum(reached[None, :] & (every[None, :] < every[:, None]), axis=1, dtype=jnp.int32)
        wanted = jnp.minimum(every, jnp.maximum(count - 1, 0))
        listed = reached[None, :] & (before[None, :] == wanted[:, None])
        order = jnp.max(jnp.where(listed, every[None, :], 0), axis=1)
        return order, count, row_at, col_at

    def extend(base, near, far, tables):
        strips = [strip for (a, b), c in zip(near, far) for strip in (a, c, b, c) * 2]
        return extend_add(base, strips, tables, r, tile)

    fence = lax.optimization_barrier
    chunks, child = fence((chunks, child))

    def gather(pieces):
        return [lax.all_gather(piece, "col", axis=0, tiled=True) for piece in pieces]

    row_chunks = gather(chunks[:1])

    ring = ((0, 2, 3, 1), (0, 1, 3, 2))
    place = chip ^ z
    half = block_rows // 2

    def device_at(c, k, plane):
        return (c * cores + k) * planes + plane

    def hand_on(held, hops):
        pairs = [
            (device_at(p ^ a, k, p), device_at(p ^ b, k, p))
            for a, b in hops
            for p in range(planes)
            for k in range(cores)
        ]
        return lax.ppermute(held, ("sub", "row", "col"), pairs)

    def halves_of(c):
        return row_chunks[c][:half], row_chunks[c][half:]

    def beat(at, got):
        taken_on = []
        for side, way in enumerate(ring):
            hops = [(way[h], way[h + 1]) for h in range(3) if 0 <= at - h < CHUNKS]
            if at < CHUNKS:
                held = halves_of(at)[side]
                if at > 0:
                    held = jnp.where(place == 0, held, got[at - 1][side])
            else:
                held = got[at - 1][side]
            taken_on.append(hand_on(held, hops))
        return got + [taken_on]

    def columns_of(c, got, straight=None):
        halves = []
        for side, (held, way) in enumerate(zip(halves_of(c), ring)):
            found = [got[c][side], got[c + 1][side]]
            found.append(got[c + 2][side] if straight is None else straight[side])
            for target, value in zip(way[1:], found):
                held = jnp.where(place == target, value, held)
            halves.append(held)
        mine = jnp.concatenate(halves, axis=0)
        return mine, xor_permute(mine, "row", rows, 1)

    local_mask = lax.dynamic_slice(
        pattern, (grid_row * tile_rows, z * tile_cols), (tile_rows, tile_cols)
    )

    def subtract(base, first, columns, in_place=True):
        mine, other = zip(*columns)
        part = row_chunks[first : first + len(columns)]
        return update(base, part, mine, other, local_mask, core, tile, in_place)

    no_turns = [0] * 4
    row_turns = no_turns[1:]
    strips = fence(send_strips())

    got = beat(0, [])
    pieces = send_columns(strips, 0)
    tables = tables_of(no_turns)
    got, pieces, chunks, tables, local_mask = fence((got, pieces, chunks, tables, local_mask))
    row_chunks = row_chunks + gather(chunks[1:])

    def first_rows(placed, turns):
        return halves_first(placed[0], turns), chips_first(placed[1], turns)

    def second_rows(first, turns):
        return chips_second(first[0], turns), halves_second(first[1], turns)

    def third_rows(near, turns):
        return [send_cores(group, turns) for group in near]

    halfway = fence(first_rows(join_columns(pieces), row_turns))

    near = second_rows(halfway, row_turns)
    got = beat(1, got)
    got, near = fence((got, near))

    far = third_rows(near, row_turns)
    got = beat(2, got)
    got, far = fence((got, far))

    columns = [columns_of(0, got)]
    base = subtract(front_trailing, 0, columns, False)
    got = beat(3, got)
    got, base = fence((got, base))

    columns.append(columns_of(1, got))
    base = extend(base, near, far, tables)
    got = beat(4, got)
    got, base, columns = fence((got, base, columns))

    columns.append(columns_of(2, got))
    base = subtract(base, 1, columns[1:2])
    got = beat(5, got)
    got, base, columns = fence((got, base, columns))

    columns.append(columns_of(3, got))
    straight = [hand_on(held, [(0, way[3])]) for held, way in zip(halves_of(5), ring)]
    got = beat(6, got)

    def more(turn, base):
        turns = turns_of(turn)
        placed = join_columns(send_columns(strips, turns[0]))
        near = second_rows(first_rows(placed, turns[1:]), turns[1:])
        return extend(base, near, third_rows(near, turns[1:]), tables_of(turns))

    every_round = functools.reduce(lambda a, b: a * b, rounds)
    base = lax.fori_loop(1, every_round, more, base)
    base = subtract(base, 2, columns[2:])
    base, got, straight = fence((base, got, straight))
    base = subtract(base, 4, [columns_of(4, got), columns_of(5, got, straight)])
    return (factor, base)


def fits_line(mesh, front_trailing, child_update, tile):
    sizes = [mesh.shape[name] for name in ("sub", "row", "col")]
    grid = sizes[0] * sizes[1]
    block_rows = front_trailing.shape[0] // grid
    block_cols = front_trailing.shape[1] // sizes[2]
    child_parts = (child_update.shape[1] // sizes[2], child_update.shape[2] // sizes[1])
    return (
        sizes == [2, 4, 4]
        and block_cols == 2 * block_rows
        and all(part % tile == 0 for part in child_parts)
        and block_rows % (4 * 2 * tile) == 0
    )


def solution(mesh):
    placed = (
        P(("sub", "row", "col"), None),
        P(),
        P(("sub", "row"), "col"),
        P("sub", "col", "row"),
        P(),
        P(),
    )

    def whole(front_panel, tile_inverse, front_trailing, child_update, child_map, pattern):
        on_line = fits_line(mesh, front_trailing, child_update, tile_inverse.shape[1])
        return jax.shard_map(
            line_device if on_line else general_device,
            mesh=mesh,
            in_specs=placed,
            out_specs=(P(("sub", "row", "col"), None), P(("sub", "row"), "col")),
            check_vma=False,
        )(front_panel, tile_inverse, front_trailing, child_update, child_map, pattern)

    return whole
```

```python
import functools
import itertools

import jax
import jax.numpy as jnp
from jax import lax
from jax.experimental import pallas as pl
from jax.experimental.pallas import tpu as pltpu
from jax.sharding import PartitionSpec as P

COL_WINDOW = 8
ROW_WINDOWS = (15, 9, 6)
MORE_COLUMNS = 2
CHUNKS = 6
VMEM = 56 * 1024 * 1024


def spread(value, axis, source):
    kept = jnp.where(lax.axis_index(axis) == source, value, 0).astype(value.dtype)
    return lax.psum(kept, axis)


def partner(value, axis, distance):
    mask = 2**distance
    pairs = [(source, source ^ mask) for source in range(lax.axis_size(axis))]
    return lax.ppermute(value, axis, pairs)


def apply_inverse(panel_rows, inverses):
    row_count = panel_rows.shape[0]
    tile_count = inverses.shape[0]
    tile_size = inverses.shape[1]
    shaped = panel_rows.reshape(row_count, tile_count, tile_size)
    scaled = jnp.einsum("rkt,kts->rks", shaped, inverses, preferred_element_type=jnp.float32)
    return scaled.astype(jnp.bfloat16).reshape(row_count, tile_count * tile_size)


def place_columns(child_block, tile_map, parent_tiles, tile_size):
    row_count = child_block.shape[0]
    tile_count = tile_map.shape[0]
    wanted = jnp.arange(parent_tiles, dtype=jnp.int32)
    onehot = (tile_map[:, None] == wanted[None, :]).astype(jnp.bfloat16)
    placed = jnp.einsum(
        "rjt,jq->rqt",
        child_block.reshape(row_count, tile_count, tile_size),
        onehot,
        preferred_element_type=jnp.float32,
    )
    return placed.astype(jnp.bfloat16).reshape(row_count, parent_tiles * tile_size)


def pick_rows(child_block, tile_map, grid_block, tile_rows, tile_size):
    tile_count = tile_map.shape[0]
    width_cols = child_block.shape[1]
    wanted = grid_block * tile_rows + jnp.arange(tile_rows, dtype=jnp.int32)
    onehot = (tile_map[:, None] == wanted[None, :]).astype(jnp.bfloat16)
    picked = jnp.einsum(
        "itx,ip->ptx",
        child_block.reshape(tile_count, tile_size, width_cols),
        onehot,
        preferred_element_type=jnp.float32,
    )
    return picked.reshape(tile_rows * tile_size, width_cols)


def general_device(front_panel, tile_inverse, front_trailing, child_update, child_map, pattern):
    tile_size = tile_inverse.shape[1]
    parent_tiles = pattern.shape[0]
    block_rows = front_trailing.shape[0]
    block_cols = front_trailing.shape[1]
    tile_rows = block_rows // tile_size
    tile_cols = block_cols // tile_size
    sub_index = lax.axis_index("sub")
    row_index = lax.axis_index("row")
    col_index = lax.axis_index("col")
    rows_count = lax.axis_size("row")
    grid_row = sub_index * rows_count + row_index
    factor = apply_inverse(front_panel, tile_inverse)
    row_panel = lax.all_gather(factor, "col", axis=0, tiled=True)
    share_rows = min(block_rows, block_cols)
    pieces = []
    for part_index in range(block_cols // share_rows):
        first_row = col_index * block_cols + part_index * share_rows
        source = first_row // block_rows
        offset = first_row % block_rows
        share_block = lax.dynamic_slice_in_dim(row_panel, offset, share_rows, 0)
        pieces.append(spread(share_block, ("sub", "row"), source))
    column_panel = pieces[0] if len(pieces) == 1 else jnp.concatenate(pieces, axis=0)
    own_map = lax.dynamic_index_in_dim(child_map, sub_index, 0, keepdims=False)
    own_child = child_update[0]
    gathered = lax.all_gather(own_child, "row", axis=1, tiled=True)
    placed = place_columns(gathered, own_map, parent_tiles, tile_size)
    child_rows = lax.all_to_all(placed, "col", split_axis=1, concat_axis=0, tiled=True)
    own_part = pick_rows(child_rows, own_map, grid_row, tile_rows, tile_size)
    other_block = (1 - sub_index) * rows_count + row_index
    sibling_part = pick_rows(child_rows, own_map, other_block, tile_rows, tile_size).astype(
        jnp.bfloat16
    )
    received = partner(sibling_part, "sub", 0)
    extend = own_part + received.astype(jnp.float32)
    local_mask = lax.dynamic_slice(
        pattern, (grid_row * tile_rows, col_index * tile_cols), (tile_rows, tile_cols)
    )
    product = lax.dot_general(
        row_panel, column_panel, (((1,), (1,)), ((), ())), preferred_element_type=jnp.float32
    )
    weights = local_mask.astype(jnp.float32)
    masked = (
        product.reshape(tile_rows, tile_size, tile_cols, tile_size) * weights[:, None, :, None]
    ).reshape(block_rows, block_cols)
    trailing = front_trailing + extend - masked
    return (factor, trailing)


def factor_kernel(panel_ref, inverse_ref, out_ref, *chunk_refs):
    count, size, _ = inverse_ref.shape
    per_chunk = count // len(chunk_refs)
    for k in range(count):
        here = (slice(None), pl.ds(k * size, size))
        scaled = jnp.dot(
            panel_ref[here], inverse_ref[k], preferred_element_type=jnp.float32
        ).astype(out_ref.dtype)
        out_ref[here] = scaled
        chunk_refs[k // per_chunk][:, pl.ds(k % per_chunk * size, size)] = scaled


def scale_panel(panel, inverses, chunks):
    rows, depth = panel.shape
    size = inverses.shape[1]
    step, wide = rows // 4, depth // chunks
    block = pl.BlockSpec((step, depth), lambda i: (i, 0))
    shape = jax.ShapeDtypeStruct
    return pl.pallas_call(
        factor_kernel,
        grid=(rows // step,),
        in_specs=[block, pl.BlockSpec(inverses.shape, lambda i: (0, 0, 0))],
        out_specs=[block] + [pl.BlockSpec((step, wide), lambda i: (i, 0))] * chunks,
        out_shape=[shape(panel.shape, panel.dtype)] + [shape((rows, wide), panel.dtype)] * chunks,
        compiler_params=pltpu.CompilerParams(vmem_limit_bytes=VMEM),
        cost_estimate=pl.CostEstimate(
            flops=2 * rows * depth * size, bytes_accessed=6 * panel.size, transcendentals=0
        ),
    )(panel, inverses)


def extend_kernel(tile, parts, groups, row_at, col_at, me, base_ref, *refs):
    strips, out_ref = refs[:-1], refs[-1]
    p = pl.program_id(0)
    part = tile // parts
    window = col_at.shape[1] // groups
    out_ref[...] = base_ref[...]
    for kid, group in itertools.product(range(2), range(groups)):

        @pl.when(row_at[kid * parts, p] >= 0)
        def _():
            @pl.loop(0, window)
            def _(b):
                q = col_at[kid, group * window + b]

                @pl.when(q >= 0)
                def _():
                    lanes = pl.ds(pl.multiple_of(q * tile, tile), tile)
                    for m in range(parts):
                        strip_ref = strips[(group * 2 + kid) * parts + m]
                        first = pl.multiple_of((me[0] ^ m) * part, part)
                        here = (pl.ds(first, part), lanes)
                        out_ref[here] += strip_ref[0, b].astype(jnp.float32)


def extend_add(base, strips, tables, me, tile, in_place):
    height, width = base.shape
    parts = tile // strips[0].shape[2]
    groups = len(strips) // (2 * parts)
    row_at, col_at = tables

    def strip_spec(i):
        return pl.BlockSpec(
            (1,) + strips[i].shape[1:],
            lambda p, row_at, *_: (jnp.maximum(row_at[i % (2 * parts), p], 0), 0, 0, 0),
        )

    block = pl.BlockSpec((tile, width), lambda p, *_: (p, 0))
    return pl.pallas_call(
        functools.partial(extend_kernel, tile, parts, groups),
        grid_spec=pltpu.PrefetchScalarGridSpec(
            num_scalar_prefetch=3,
            grid=(height // tile,),
            in_specs=[block] + [strip_spec(i) for i in range(len(strips))],
            out_specs=block,
        ),
        out_shape=jax.ShapeDtypeStruct(base.shape, base.dtype),
        input_output_aliases={3: 0} if in_place else {},
        compiler_params=pltpu.CompilerParams(vmem_limit_bytes=VMEM),
        cost_estimate=pl.CostEstimate(
            flops=base.size, bytes_accessed=8 * base.size, transcendentals=0
        ),
    )(row_at, col_at, me.reshape(1), base, *strips)


def update_kernel(tile, count, core, mask, *refs):
    rows, mine, other = (refs[k * count : (k + 1) * count] for k in range(3))
    base_ref, out_ref = refs[3 * count :]
    i, c = pl.program_id(0), pl.program_id(1)
    high, wide = out_ref.shape[0] // tile, out_ref.shape[1] // tile
    per_side = pl.num_programs(1) // 2
    first = column_block(c, per_side, core) * wide
    for side, cols in enumerate((mine, other)):

        @pl.when(c // per_side == side)
        def _():
            for q in range(wide):
                lanes = pl.ds(q * tile, tile)
                product = sum(
                    lax.dot_general(
                        rows_ref[...],
                        cols_ref[lanes, :],
                        (((1,), (1,)), ((), ())),
                        preferred_element_type=jnp.float32,
                    )
                    for rows_ref, cols_ref in zip(rows, cols)
                )
                for a in range(high):
                    here = (pl.ds(a * tile, tile), lanes)
                    reached = mask[i * high + a, first + q].astype(jnp.float32)
                    part = product[a * tile : (a + 1) * tile]
                    out_ref[here] = base_ref[here] - reached * part


def column_block(c, per_side, core):
    return (c // per_side ^ core[0]) * per_side + c % per_side


def update(base, rows, mine, other, mask, core, tile):
    height, width = base.shape
    step = 2 * tile
    per_side = width // step // 2
    block = pl.BlockSpec((height, step), lambda i, c, core, _: (i, column_block(c, per_side, core)))
    row_block = lambda i, c, *_: (i, 0)
    mine_block = lambda i, c, *_: (jnp.minimum(c, per_side - 1), 0)
    other_block = lambda i, c, *_: (jnp.maximum(c - per_side, 0), 0)
    specs = [
        pl.BlockSpec((size, piece.shape[1]), at)
        for pieces, size, at in (
            (rows, height, row_block),
            (mine, step, mine_block),
            (other, step, other_block),
        )
        for piece in pieces
    ]
    depth = sum(piece.shape[1] for piece in rows)
    return pl.pallas_call(
        functools.partial(update_kernel, tile, len(rows)),
        grid_spec=pltpu.PrefetchScalarGridSpec(
            num_scalar_prefetch=2,
            grid=(1, width // step),
            in_specs=specs + [block],
            out_specs=block,
        ),
        out_shape=jax.ShapeDtypeStruct(base.shape, base.dtype),
        input_output_aliases={2 + 3 * len(rows): 0},
        compiler_params=pltpu.CompilerParams(vmem_limit_bytes=VMEM),
        cost_estimate=pl.CostEstimate(
            flops=2 * height * width * depth, bytes_accessed=8 * base.size, transcendentals=0
        ),
    )(core.reshape(1), mask, *rows, *mine, *other, base)


def xor_permute(value, axes, size, mask):
    if mask == 0:
        return value
    return lax.ppermute(value, axes, [(i, i ^ mask) for i in range(size)])


def line_device(front_panel, tile_inverse, front_trailing, child_update, child_map, pattern):
    tile = tile_inverse.shape[1]
    block_rows, block_cols = front_trailing.shape
    tile_rows, tile_cols = block_rows // tile, block_cols // tile
    subs, rows, planes = (lax.axis_size(name) for name in ("sub", "row", "col"))
    grid = subs * rows
    cores = 2
    plane_axes = ("sub", "row")
    s, r, z = (lax.axis_index(name) for name in ("sub", "row", "col"))
    grid_row = s * rows + r
    chip, core = grid_row // cores, grid_row % cores
    shard = front_panel.shape[0]

    factor, *chunks = scale_panel(front_panel, tile_inverse, CHUNKS)

    child = child_update[0]
    own_rows, own_cols = child.shape[0] // tile, child.shape[1] // tile
    child_tiles = child_map.shape[1]
    part = tile // rows
    def send_strips():
        shaped = child.reshape(own_rows, rows, part, own_cols, tile).transpose(1, 0, 3, 2, 4)
        return [
            xor_permute(
                lax.dynamic_index_in_dim(shaped, r ^ m, 0, keepdims=False), "row", rows, m
            )
            for m in range(rows)
        ]

    def edges_of(count):
        first = jnp.arange(count + 1, dtype=jnp.int32) * (pattern.shape[0] // count)
        return (child_map[:, None, :] < first[None, :, None]).sum(-1, dtype=jnp.int32)

    def rounds_of(edges, size):
        return (jnp.max(edges[:, 1:] - edges[:, :-1]) + size - 1) // size

    col_edges = edges_of(planes)
    row_edges = [edges_of(count) for count in (subs, subs * rows // cores, grid)]
    def turns_of(turn, rounds):
        turns = []
        for count in reversed(rounds):
            turns.append(turn % count)
            turn = turn // count
        return turns[::-1]

    kids = (s, 1 - s)

    def router(col_base, col_window, row_windows):
        def col_start(kid, plane, turn):
            return jnp.minimum(col_edges[kid, plane] + col_base + turn * col_window, child_tiles - col_window)

        def row_starts(kid, row, turns):
            start, size, found = 0, child_tiles, []
            places_at = (row // rows, row // cores, row)
            for edges, at, turn, window in zip(row_edges, places_at, turns, row_windows):
                start = jnp.clip(edges[kid, at] + turn * window, start, start + size - window)
                size = window
                found.append(start)
            return found

        def send_columns(strips, turn):
            stripped = jnp.zeros((own_rows, child_tiles, part, tile), child.dtype)
            for m, got in enumerate(strips):
                stripped = lax.dynamic_update_slice(stripped, got, (0, (r ^ m) * own_cols, 0, 0))
            pieces = []
            for m in range(planes):
                start = col_start(s, z ^ m, turn)
                piece = lax.dynamic_slice_in_dim(stripped, start, col_window, 1)
                pieces.append(xor_permute(piece, "col", planes, m))
            return pieces

        def join_columns(pieces):
            groups = []
            for half in range(2):
                placed = jnp.zeros((child_tiles, col_window // 2, part, tile), child.dtype)
                for m, got in enumerate(pieces):
                    got = got[:, half * col_window // 2 : (half + 1) * col_window // 2]
                    placed = lax.dynamic_update_slice(placed, got, ((z ^ m) * own_rows, 0, 0, 0))
                groups.append(placed)
            return groups

        def taken(value, start, size):
            return lax.dynamic_slice_in_dim(value, start, size, 0)

        size = row_windows[1]

        def rows_for(values, row, turns, level=None):
            parts = []
            for value, kid in zip(values, kids):
                found = row_starts(kid, row, turns)
                first = 0 if level is None else found[level]
                parts.append(taken(value, found[1] - first, size))
            return parts

        def halves_first(placed, turns):
            here, there = (row_starts(s, row, turns)[0] for row in (grid_row, grid_row ^ rows))
            window = row_windows[0]
            return [
                taken(placed, here, window),
                xor_permute(taken(placed, there, window), "sub", subs, 1),
            ]

        def chips_second(halves, turns):
            here, there = (
                jnp.concatenate(rows_for(halves, row, turns, 0), axis=0)
                for row in (grid_row, grid_row ^ cores)
            )
            return [here, xor_permute(there, "row", rows, cores)]

        def chips_first(placed, turns):
            def of_both_halves(row):
                found = [rows_for([placed], half * rows + row, turns)[0] for half in range(subs)]
                return jnp.concatenate(found, axis=0)

            return [of_both_halves(r), xor_permute(of_both_halves(r ^ cores), "row", rows, cores)]

        def halves_second(strips, turns):
            here, there = (
                [taken(strip, half * size, size) for strip in strips] for half in kids
            )
            got = xor_permute(jnp.concatenate(there, axis=0), "sub", subs, 1)
            return [
                jnp.concatenate((kept, got[k * size : (k + 1) * size]), axis=0)
                for k, kept in enumerate(here)
            ]

        def send_cores(strips, turns):
            found = [row_starts(kid, grid_row ^ 1, turns) for kid in kids]
            parts = [
                taken(strip, kid * size + at[2] - at[1], row_windows[2])
                for strip in strips
                for kid, at in enumerate(found)
            ]
            return xor_permute(jnp.concatenate(parts, axis=0), "row", rows, 1)

        def tables_of(turns):
            col_turn, row_turns = turns[0], turns[1:]
            col_at, row_at = [], []
            wanted = grid_row * tile_rows + jnp.arange(tile_rows, dtype=jnp.int32)
            for place, kid in enumerate(kids):
                own_map = lax.dynamic_index_in_dim(child_map, kid, 0, keepdims=False)
                first = col_edges[kid, z] + col_base + col_turn * col_window
                last = jnp.minimum(first + col_window, col_edges[kid, z + 1])
                start = col_start(kid, z, col_turn)
                slot = start + jnp.arange(col_window, dtype=jnp.int32)
                parent = lax.dynamic_slice_in_dim(own_map, start, col_window) - z * tile_cols
                col_at.append(jnp.where((slot >= first) & (slot < last), parent, -1))

                same = own_map[None, :] == wanted[:, None]
                slot = jnp.max(jnp.where(same, jnp.arange(child_tiles, dtype=jnp.int32), -1), axis=1)
                held = slot >= 0
                at_level = (s, chip, grid_row)
                for edges, at, turn, window in zip(row_edges, at_level, row_turns, row_windows):
                    first = edges[kid, at] + turn * window
                    held &= (slot >= first) & (slot < first + window)
                starts = row_starts(kid, grid_row, row_turns)
                near_at = place * row_windows[1] + slot - starts[1]
                far_at = [(k * 2 + place) * row_windows[2] + slot - starts[2] for k in range(2)]
                order = (near_at, far_at[0], near_at, far_at[1])
                row_at += [jnp.where(held, at, -1) for at in order]
            return jnp.stack(row_at), jnp.stack(col_at)

        def first_rows(placed, turns):
            return halves_first(placed[0], turns), chips_first(placed[1], turns)

        def second_rows(first, turns):
            return chips_second(first[0], turns), halves_second(first[1], turns)

        def third_rows(near, turns):
            return [send_cores(group, turns) for group in near]
        return send_columns, join_columns, first_rows, second_rows, third_rows, tables_of

    def extend(base, near, far, tables, in_place=True):
        strips = [strip for (a, b), c in zip(near, far) for strip in (a, c, b, c) * 2]
        return extend_add(base, strips, tables, r, tile, in_place)

    fence = lax.optimization_barrier
    chunks, child = fence((chunks, child))

    def gather(pieces):
        return [lax.all_gather(piece, "col", axis=0, tiled=True) for piece in pieces]

    row_chunks = gather(chunks[:1])

    ring = ((0, 2, 3, 1), (0, 1, 3, 2))
    place = chip ^ z
    half = block_rows // 2

    def device_at(c, k, plane):
        return (c * cores + k) * planes + plane

    def hand_on(held, hops):
        pairs = [
            (device_at(p ^ a, k, p), device_at(p ^ b, k, p))
            for a, b in hops
            for p in range(planes)
            for k in range(cores)
        ]
        return lax.ppermute(held, ("sub", "row", "col"), pairs)

    def halves_of(c):
        return row_chunks[c][:half], row_chunks[c][half:]

    def beat(at, got):
        taken_on = []
        for side, way in enumerate(ring):
            hops = [(way[h], way[h + 1]) for h in range(3) if 0 <= at - h < CHUNKS]
            if at < CHUNKS:
                held = halves_of(at)[side]
                if at > 0:
                    held = jnp.where(place == 0, held, got[at - 1][side])
            else:
                held = got[at - 1][side]
            taken_on.append(hand_on(held, hops))
        return got + [taken_on]

    def columns_of(c, got, straight=None):
        halves = []
        for side, (held, way) in enumerate(zip(halves_of(c), ring)):
            found = [got[c][side], got[c + 1][side]]
            found.append(got[c + 2][side] if straight is None else straight[side])
            for target, value in zip(way[1:], found):
                held = jnp.where(place == target, value, held)
            halves.append(held)
        mine = jnp.concatenate(halves, axis=0)
        return mine, xor_permute(mine, "row", rows, 1)

    local_mask = lax.dynamic_slice(
        pattern, (grid_row * tile_rows, z * tile_cols), (tile_rows, tile_cols)
    )

    def subtract(base, first, columns):
        mine, other = zip(*columns)
        part = row_chunks[first : first + len(columns)]
        return update(base, part, mine, other, local_mask, core, tile)

    no_turns = [0] * 4
    row_turns = no_turns[1:]
    strips = fence(send_strips())

    col_window = min(COL_WINDOW, child_tiles)
    row_windows = [min(size, child_tiles) for size in ROW_WINDOWS]
    send_columns, join_columns, first_rows, second_rows, third_rows, tables_of = router(
        0, col_window, row_windows
    )
    got = beat(0, [])
    pieces = send_columns(strips, 0)
    tables = tables_of(no_turns)
    got, pieces, chunks, tables, local_mask = fence((got, pieces, chunks, tables, local_mask))
    row_chunks = row_chunks + gather(chunks[1:])

    placed = join_columns(pieces)
    halfway = first_rows(placed, row_turns)
    got = beat(1, got)
    got, halfway = fence((got, halfway))

    near = second_rows(halfway, row_turns)
    got, near, row_chunks[2] = fence((got, near, row_chunks[2]))

    got = beat(2, got)
    far = third_rows(near, row_turns)
    base = extend(front_trailing, near, far, tables, False)
    got = beat(4, beat(3, got))
    columns = [columns_of(c, got) for c in (0, 1)]
    got, base, columns, row_chunks[5] = fence((got, base, columns, row_chunks[5]))

    row_rounds = [rounds_of(edges, size) for edges, size in zip(row_edges, row_windows)]
    every_round = functools.reduce(lambda a, b: a * b, row_rounds)

    def more_rows(turn, base):
        turns = turns_of(turn, row_rounds)
        near = second_rows(first_rows(placed, turns), turns)
        return extend(base, near, third_rows(near, turns), tables_of([0] + turns))

    base = lax.fori_loop(1, every_round, more_rows, base)

    most = jnp.max(col_edges[:, 1:] - col_edges[:, :-1])
    ranges = [pattern.shape[0] // count for count in (subs, subs * rows // cores, grid)]
    sends, joins, firsts, seconds, thirds, tables_at = router(
        col_window, MORE_COLUMNS, [min(size, child_tiles) for size in ranges]
    )

    def more_columns(turn, base):
        near = seconds(firsts(joins(sends(strips, turn)), row_turns), row_turns)
        return extend(base, near, thirds(near, row_turns), tables_at([turn] + row_turns))

    left = jnp.maximum(most - col_window, 0)
    base = lax.fori_loop(0, (left + MORE_COLUMNS - 1) // MORE_COLUMNS, more_columns, base)

    base = subtract(base, 0, columns)
    columns = [columns_of(2, got)]
    got = beat(5, got)
    got, base, columns = fence((got, base, columns))

    base = subtract(base, 2, columns)
    straight = [hand_on(held, [(0, way[3])]) for held, way in zip(halves_of(5), ring)]
    got = beat(6, got)

    base, got, straight = fence((base, got, straight))
    columns = [columns_of(3, got), columns_of(4, got), columns_of(5, got, straight)]
    base = subtract(base, 3, columns)
    return (factor, base)


def fits_line(mesh, front_trailing, child_update, tile):
    sizes = [mesh.shape[name] for name in ("sub", "row", "col")]
    grid = sizes[0] * sizes[1]
    block_rows = front_trailing.shape[0] // grid
    block_cols = front_trailing.shape[1] // sizes[2]
    child_parts = (child_update.shape[1] // sizes[2], child_update.shape[2] // sizes[1])
    return (
        sizes == [2, 4, 4]
        and block_cols == 2 * block_rows
        and all(part % tile == 0 for part in child_parts)
        and block_rows % (4 * 2 * tile) == 0
    )


def solution(mesh):
    placed = (
        P(("sub", "row", "col"), None),
        P(),
        P(("sub", "row"), "col"),
        P("sub", "col", "row"),
        P(),
        P(),
    )

    def whole(front_panel, tile_inverse, front_trailing, child_update, child_map, pattern):
        on_line = fits_line(mesh, front_trailing, child_update, tile_inverse.shape[1])
        return jax.shard_map(
            line_device if on_line else general_device,
            mesh=mesh,
            in_specs=placed,
            out_specs=(P(("sub", "row", "col"), None), P(("sub", "row"), "col")),
            check_vma=False,
        )(front_panel, tile_inverse, front_trailing, child_update, child_map, pattern)

    return whole
```

```python
import functools
import itertools

import jax
import jax.numpy as jnp
from jax import lax
from jax.experimental import pallas as pl
from jax.experimental.pallas import tpu as pltpu
from jax.sharding import PartitionSpec as P

COL_WINDOW = 8
ROW_WINDOWS = (15, 9, 6)
MORE_COLUMNS = 2
CHUNKS = 6
VMEM = 56 * 1024 * 1024


def spread(value, axis, source):
    kept = jnp.where(lax.axis_index(axis) == source, value, 0).astype(value.dtype)
    return lax.psum(kept, axis)


def partner(value, axis, distance):
    mask = 2**distance
    pairs = [(source, source ^ mask) for source in range(lax.axis_size(axis))]
    return lax.ppermute(value, axis, pairs)


def apply_inverse(panel_rows, inverses):
    row_count = panel_rows.shape[0]
    tile_count = inverses.shape[0]
    tile_size = inverses.shape[1]
    shaped = panel_rows.reshape(row_count, tile_count, tile_size)
    scaled = jnp.einsum("rkt,kts->rks", shaped, inverses, preferred_element_type=jnp.float32)
    return scaled.astype(jnp.bfloat16).reshape(row_count, tile_count * tile_size)


def place_columns(child_block, tile_map, parent_tiles, tile_size):
    row_count = child_block.shape[0]
    tile_count = tile_map.shape[0]
    wanted = jnp.arange(parent_tiles, dtype=jnp.int32)
    onehot = (tile_map[:, None] == wanted[None, :]).astype(jnp.bfloat16)
    placed = jnp.einsum(
        "rjt,jq->rqt",
        child_block.reshape(row_count, tile_count, tile_size),
        onehot,
        preferred_element_type=jnp.float32,
    )
    return placed.astype(jnp.bfloat16).reshape(row_count, parent_tiles * tile_size)


def pick_rows(child_block, tile_map, grid_block, tile_rows, tile_size):
    tile_count = tile_map.shape[0]
    width_cols = child_block.shape[1]
    wanted = grid_block * tile_rows + jnp.arange(tile_rows, dtype=jnp.int32)
    onehot = (tile_map[:, None] == wanted[None, :]).astype(jnp.bfloat16)
    picked = jnp.einsum(
        "itx,ip->ptx",
        child_block.reshape(tile_count, tile_size, width_cols),
        onehot,
        preferred_element_type=jnp.float32,
    )
    return picked.reshape(tile_rows * tile_size, width_cols)


def general_device(front_panel, tile_inverse, front_trailing, child_update, child_map, pattern):
    tile_size = tile_inverse.shape[1]
    parent_tiles = pattern.shape[0]
    block_rows = front_trailing.shape[0]
    block_cols = front_trailing.shape[1]
    tile_rows = block_rows // tile_size
    tile_cols = block_cols // tile_size
    sub_index = lax.axis_index("sub")
    row_index = lax.axis_index("row")
    col_index = lax.axis_index("col")
    rows_count = lax.axis_size("row")
    grid_row = sub_index * rows_count + row_index
    factor = apply_inverse(front_panel, tile_inverse)
    row_panel = lax.all_gather(factor, "col", axis=0, tiled=True)
    share_rows = min(block_rows, block_cols)
    pieces = []
    for part_index in range(block_cols // share_rows):
        first_row = col_index * block_cols + part_index * share_rows
        source = first_row // block_rows
        offset = first_row % block_rows
        share_block = lax.dynamic_slice_in_dim(row_panel, offset, share_rows, 0)
        pieces.append(spread(share_block, ("sub", "row"), source))
    column_panel = pieces[0] if len(pieces) == 1 else jnp.concatenate(pieces, axis=0)
    own_map = lax.dynamic_index_in_dim(child_map, sub_index, 0, keepdims=False)
    own_child = child_update[0]
    gathered = lax.all_gather(own_child, "row", axis=1, tiled=True)
    placed = place_columns(gathered, own_map, parent_tiles, tile_size)
    child_rows = lax.all_to_all(placed, "col", split_axis=1, concat_axis=0, tiled=True)
    own_part = pick_rows(child_rows, own_map, grid_row, tile_rows, tile_size)
    other_block = (1 - sub_index) * rows_count + row_index
    sibling_part = pick_rows(child_rows, own_map, other_block, tile_rows, tile_size).astype(
        jnp.bfloat16
    )
    received = partner(sibling_part, "sub", 0)
    extend = own_part + received.astype(jnp.float32)
    local_mask = lax.dynamic_slice(
        pattern, (grid_row * tile_rows, col_index * tile_cols), (tile_rows, tile_cols)
    )
    product = lax.dot_general(
        row_panel, column_panel, (((1,), (1,)), ((), ())), preferred_element_type=jnp.float32
    )
    weights = local_mask.astype(jnp.float32)
    masked = (
        product.reshape(tile_rows, tile_size, tile_cols, tile_size) * weights[:, None, :, None]
    ).reshape(block_rows, block_cols)
    trailing = front_trailing + extend - masked
    return (factor, trailing)


def factor_kernel(panel_ref, inverse_ref, out_ref, *chunk_refs):
    count, size, _ = inverse_ref.shape
    per_chunk = count // len(chunk_refs)
    for k in range(count):
        here = (slice(None), pl.ds(k * size, size))
        scaled = jnp.dot(
            panel_ref[here], inverse_ref[k], preferred_element_type=jnp.float32
        ).astype(out_ref.dtype)
        out_ref[here] = scaled
        chunk_refs[k // per_chunk][:, pl.ds(k % per_chunk * size, size)] = scaled


def scale_panel(panel, inverses, chunks):
    rows, depth = panel.shape
    size = inverses.shape[1]
    step, wide = rows // 4, depth // chunks
    block = pl.BlockSpec((step, depth), lambda i: (i, 0))
    shape = jax.ShapeDtypeStruct
    return pl.pallas_call(
        factor_kernel,
        grid=(rows // step,),
        in_specs=[block, pl.BlockSpec(inverses.shape, lambda i: (0, 0, 0))],
        out_specs=[block] + [pl.BlockSpec((step, wide), lambda i: (i, 0))] * chunks,
        out_shape=[shape(panel.shape, panel.dtype)] + [shape((rows, wide), panel.dtype)] * chunks,
        compiler_params=pltpu.CompilerParams(vmem_limit_bytes=VMEM),
        cost_estimate=pl.CostEstimate(
            flops=2 * rows * depth * size, bytes_accessed=6 * panel.size, transcendentals=0
        ),
    )(panel, inverses)


def extend_kernel(tile, parts, groups, row_at, col_at, me, base_ref, *refs):
    strips, out_ref = refs[:-1], refs[-1]
    p = pl.program_id(0)
    part = tile // parts
    window = col_at.shape[1] // groups
    out_ref[...] = base_ref[...]
    for kid, group in itertools.product(range(2), range(groups)):

        @pl.when(row_at[kid * parts, p] >= 0)
        def _():
            @pl.loop(0, window)
            def _(b):
                q = col_at[kid, group * window + b]

                @pl.when(q >= 0)
                def _():
                    lanes = pl.ds(pl.multiple_of(q * tile, tile), tile)
                    for m in range(parts):
                        strip_ref = strips[(group * 2 + kid) * parts + m]
                        first = pl.multiple_of((me[0] ^ m) * part, part)
                        here = (pl.ds(first, part), lanes)
                        out_ref[here] += strip_ref[0, b].astype(jnp.float32)


def extend_add(base, strips, tables, me, tile, in_place):
    height, width = base.shape
    parts = tile // strips[0].shape[2]
    groups = len(strips) // (2 * parts)
    row_at, col_at = tables

    def strip_spec(i):
        return pl.BlockSpec(
            (1,) + strips[i].shape[1:],
            lambda p, row_at, *_: (jnp.maximum(row_at[i % (2 * parts), p], 0), 0, 0, 0),
        )

    block = pl.BlockSpec((tile, width), lambda p, *_: (p, 0))
    return pl.pallas_call(
        functools.partial(extend_kernel, tile, parts, groups),
        grid_spec=pltpu.PrefetchScalarGridSpec(
            num_scalar_prefetch=3,
            grid=(height // tile,),
            in_specs=[block] + [strip_spec(i) for i in range(len(strips))],
            out_specs=block,
        ),
        out_shape=jax.ShapeDtypeStruct(base.shape, base.dtype),
        input_output_aliases={3: 0} if in_place else {},
        compiler_params=pltpu.CompilerParams(vmem_limit_bytes=VMEM),
        cost_estimate=pl.CostEstimate(
            flops=base.size, bytes_accessed=8 * base.size, transcendentals=0
        ),
    )(row_at, col_at, me.reshape(1), base, *strips)


def update_kernel(tile, count, core, mask, *refs):
    rows, mine, other = (refs[k * count : (k + 1) * count] for k in range(3))
    base_ref, out_ref = refs[3 * count :]
    i, c = pl.program_id(0), pl.program_id(1)
    high, wide = out_ref.shape[0] // tile, out_ref.shape[1] // tile
    per_side = pl.num_programs(1) // 2
    first = column_block(c, per_side, core) * wide
    for side, cols in enumerate((mine, other)):

        @pl.when(c // per_side == side)
        def _():
            for q in range(wide):
                lanes = pl.ds(q * tile, tile)
                product = sum(
                    lax.dot_general(
                        rows_ref[...],
                        cols_ref[lanes, :],
                        (((1,), (1,)), ((), ())),
                        preferred_element_type=jnp.float32,
                    )
                    for rows_ref, cols_ref in zip(rows, cols)
                )
                for a in range(high):
                    here = (pl.ds(a * tile, tile), lanes)
                    reached = mask[i * high + a, first + q].astype(jnp.float32)
                    part = product[a * tile : (a + 1) * tile]
                    out_ref[here] = base_ref[here] - reached * part


def column_block(c, per_side, core):
    return (c // per_side ^ core[0]) * per_side + c % per_side


def update(base, rows, mine, other, mask, core, tile):
    height, width = base.shape
    step = 2 * tile
    per_side = width // step // 2
    block = pl.BlockSpec((height, step), lambda i, c, core, _: (i, column_block(c, per_side, core)))
    row_block = lambda i, c, *_: (i, 0)
    mine_block = lambda i, c, *_: (jnp.minimum(c, per_side - 1), 0)
    other_block = lambda i, c, *_: (jnp.maximum(c - per_side, 0), 0)
    specs = [
        pl.BlockSpec((size, piece.shape[1]), at)
        for pieces, size, at in (
            (rows, height, row_block),
            (mine, step, mine_block),
            (other, step, other_block),
        )
        for piece in pieces
    ]
    depth = sum(piece.shape[1] for piece in rows)
    return pl.pallas_call(
        functools.partial(update_kernel, tile, len(rows)),
        grid_spec=pltpu.PrefetchScalarGridSpec(
            num_scalar_prefetch=2,
            grid=(1, width // step),
            in_specs=specs + [block],
            out_specs=block,
        ),
        out_shape=jax.ShapeDtypeStruct(base.shape, base.dtype),
        input_output_aliases={2 + 3 * len(rows): 0},
        compiler_params=pltpu.CompilerParams(vmem_limit_bytes=VMEM),
        cost_estimate=pl.CostEstimate(
            flops=2 * height * width * depth, bytes_accessed=8 * base.size, transcendentals=0
        ),
    )(core.reshape(1), mask, *rows, *mine, *other, base)


def xor_permute(value, axes, size, mask):
    if mask == 0:
        return value
    return lax.ppermute(value, axes, [(i, i ^ mask) for i in range(size)])


def line_device(front_panel, tile_inverse, front_trailing, child_update, child_map, pattern):
    tile = tile_inverse.shape[1]
    block_rows, block_cols = front_trailing.shape
    tile_rows, tile_cols = block_rows // tile, block_cols // tile
    subs, rows, planes = (lax.axis_size(name) for name in ("sub", "row", "col"))
    grid = subs * rows
    cores = 2
    plane_axes = ("sub", "row")
    s, r, z = (lax.axis_index(name) for name in ("sub", "row", "col"))
    grid_row = s * rows + r
    chip, core = grid_row // cores, grid_row % cores
    shard = front_panel.shape[0]

    factor, *chunks = scale_panel(front_panel, tile_inverse, CHUNKS)

    child = child_update[0]
    own_rows, own_cols = child.shape[0] // tile, child.shape[1] // tile
    child_tiles = child_map.shape[1]
    part = tile // rows
    def send_strips():
        shaped = child.reshape(own_rows, rows, part, own_cols, tile).transpose(1, 0, 3, 2, 4)
        return [
            xor_permute(
                lax.dynamic_index_in_dim(shaped, r ^ m, 0, keepdims=False), "row", rows, m
            )
            for m in range(rows)
        ]

    def edges_of(count):
        first = jnp.arange(count + 1, dtype=jnp.int32) * (pattern.shape[0] // count)
        return (child_map[:, None, :] < first[None, :, None]).sum(-1, dtype=jnp.int32)

    def rounds_of(edges, size):
        return (jnp.max(edges[:, 1:] - edges[:, :-1]) + size - 1) // size

    col_edges = edges_of(planes)
    row_edges = [edges_of(count) for count in (subs, subs * rows // cores, grid)]
    def turns_of(turn, rounds):
        turns = []
        for count in reversed(rounds):
            turns.append(turn % count)
            turn = turn // count
        return turns[::-1]

    kids = (s, 1 - s)

    def router(col_base, col_window, row_windows):
        def col_start(kid, plane, turn):
            return jnp.minimum(col_edges[kid, plane] + col_base + turn * col_window, child_tiles - col_window)

        def row_starts(kid, row, turns):
            start, size, found = 0, child_tiles, []
            places_at = (row // rows, row // cores, row)
            for edges, at, turn, window in zip(row_edges, places_at, turns, row_windows):
                start = jnp.clip(edges[kid, at] + turn * window, start, start + size - window)
                size = window
                found.append(start)
            return found

        def send_columns(strips, turn):
            stripped = jnp.zeros((own_rows, child_tiles, part, tile), child.dtype)
            for m, got in enumerate(strips):
                stripped = lax.dynamic_update_slice(stripped, got, (0, (r ^ m) * own_cols, 0, 0))
            pieces = []
            for m in range(planes):
                start = col_start(s, z ^ m, turn)
                piece = lax.dynamic_slice_in_dim(stripped, start, col_window, 1)
                pieces.append(xor_permute(piece, "col", planes, m))
            return pieces

        def join_columns(pieces):
            groups = []
            for half in range(2):
                placed = jnp.zeros((child_tiles, col_window // 2, part, tile), child.dtype)
                for m, got in enumerate(pieces):
                    got = got[:, half * col_window // 2 : (half + 1) * col_window // 2]
                    placed = lax.dynamic_update_slice(placed, got, ((z ^ m) * own_rows, 0, 0, 0))
                groups.append(placed)
            return groups

        def taken(value, start, size):
            return lax.dynamic_slice_in_dim(value, start, size, 0)

        size = row_windows[1]

        def rows_for(values, row, turns, level=None):
            parts = []
            for value, kid in zip(values, kids):
                found = row_starts(kid, row, turns)
                first = 0 if level is None else found[level]
                parts.append(taken(value, found[1] - first, size))
            return parts

        def halves_first(placed, turns):
            here, there = (row_starts(s, row, turns)[0] for row in (grid_row, grid_row ^ rows))
            window = row_windows[0]
            return [
                taken(placed, here, window),
                xor_permute(taken(placed, there, window), "sub", subs, 1),
            ]

        def chips_second(halves, turns):
            here, there = (
                jnp.concatenate(rows_for(halves, row, turns, 0), axis=0)
                for row in (grid_row, grid_row ^ cores)
            )
            return [here, xor_permute(there, "row", rows, cores)]

        def chips_first(placed, turns):
            def of_both_halves(row):
                found = [rows_for([placed], half * rows + row, turns)[0] for half in range(subs)]
                return jnp.concatenate(found, axis=0)

            return [of_both_halves(r), xor_permute(of_both_halves(r ^ cores), "row", rows, cores)]

        def halves_second(strips, turns):
            here, there = (
                [taken(strip, half * size, size) for strip in strips] for half in kids
            )
            got = xor_permute(jnp.concatenate(there, axis=0), "sub", subs, 1)
            return [
                jnp.concatenate((kept, got[k * size : (k + 1) * size]), axis=0)
                for k, kept in enumerate(here)
            ]

        def send_cores(strips, turns):
            found = [row_starts(kid, grid_row ^ 1, turns) for kid in kids]
            parts = [
                taken(strip, kid * size + at[2] - at[1], row_windows[2])
                for strip in strips
                for kid, at in enumerate(found)
            ]
            return xor_permute(jnp.concatenate(parts, axis=0), "row", rows, 1)

        def tables_of(turns):
            col_turn, row_turns = turns[0], turns[1:]
            col_at, row_at = [], []
            wanted = grid_row * tile_rows + jnp.arange(tile_rows, dtype=jnp.int32)
            for place, kid in enumerate(kids):
                own_map = lax.dynamic_index_in_dim(child_map, kid, 0, keepdims=False)
                first = col_edges[kid, z] + col_base + col_turn * col_window
                last = jnp.minimum(first + col_window, col_edges[kid, z + 1])
                start = col_start(kid, z, col_turn)
                slot = start + jnp.arange(col_window, dtype=jnp.int32)
                parent = lax.dynamic_slice_in_dim(own_map, start, col_window) - z * tile_cols
                col_at.append(jnp.where((slot >= first) & (slot < last), parent, -1))

                same = own_map[None, :] == wanted[:, None]
                slot = jnp.max(jnp.where(same, jnp.arange(child_tiles, dtype=jnp.int32), -1), axis=1)
                held = slot >= 0
                at_level = (s, chip, grid_row)
                for edges, at, turn, window in zip(row_edges, at_level, row_turns, row_windows):
                    first = edges[kid, at] + turn * window
                    held &= (slot >= first) & (slot < first + window)
                starts = row_starts(kid, grid_row, row_turns)
                near_at = place * row_windows[1] + slot - starts[1]
                far_at = [(k * 2 + place) * row_windows[2] + slot - starts[2] for k in range(2)]
                order = (near_at, far_at[0], near_at, far_at[1])
                row_at += [jnp.where(held, at, -1) for at in order]
            return jnp.stack(row_at), jnp.stack(col_at)

        def first_rows(placed, turns):
            return halves_first(placed[0], turns), chips_first(placed[1], turns)

        def second_rows(first, turns):
            return chips_second(first[0], turns), halves_second(first[1], turns)

        def third_rows(near, turns):
            return [send_cores(group, turns) for group in near]
        return send_columns, join_columns, first_rows, second_rows, third_rows, tables_of

    def extend(base, near, far, tables, in_place=True):
        strips = [strip for (a, b), c in zip(near, far) for strip in (a, c, b, c) * 2]
        return extend_add(base, strips, tables, r, tile, in_place)

    fence = lax.optimization_barrier
    chunks, child = fence((chunks, child))

    def gather(pieces):
        return [lax.all_gather(piece, "col", axis=0, tiled=True) for piece in pieces]

    row_chunks = gather(chunks[:1])

    ring = ((0, 2, 3, 1), (0, 1, 3, 2))
    place = chip ^ z
    half = block_rows // 2

    def device_at(c, k, plane):
        return (c * cores + k) * planes + plane

    def hand_on(held, hops):
        pairs = [
            (device_at(p ^ a, k, p), device_at(p ^ b, k, p))
            for a, b in hops
            for p in range(planes)
            for k in range(cores)
        ]
        return lax.ppermute(held, ("sub", "row", "col"), pairs)

    def halves_of(c):
        return row_chunks[c][:half], row_chunks[c][half:]

    def beat(at, got):
        taken_on = []
        for side, way in enumerate(ring):
            hops = [(way[h], way[h + 1]) for h in range(3) if 0 <= at - h < CHUNKS]
            if at < CHUNKS:
                held = halves_of(at)[side]
                if at > 0:
                    held = jnp.where(place == 0, held, got[at - 1][side])
            else:
                held = got[at - 1][side]
            taken_on.append(hand_on(held, hops))
        return got + [taken_on]

    def columns_of(c, got, straight=None):
        halves = []
        for side, (held, way) in enumerate(zip(halves_of(c), ring)):
            found = [got[c][side], got[c + 1][side]]
            found.append(got[c + 2][side] if straight is None else straight[side])
            for target, value in zip(way[1:], found):
                held = jnp.where(place == target, value, held)
            halves.append(held)
        mine = jnp.concatenate(halves, axis=0)
        return mine, xor_permute(mine, "row", rows, 1)

    local_mask = lax.dynamic_slice(
        pattern, (grid_row * tile_rows, z * tile_cols), (tile_rows, tile_cols)
    )

    def subtract(base, first, columns):
        mine, other = zip(*columns)
        part = row_chunks[first : first + len(columns)]
        return update(base, part, mine, other, local_mask, core, tile)

    no_turns = [0] * 4
    row_turns = no_turns[1:]
    strips = fence(send_strips())

    col_window = min(COL_WINDOW, child_tiles)
    row_windows = [min(size, child_tiles) for size in ROW_WINDOWS]
    send_columns, join_columns, first_rows, second_rows, third_rows, tables_of = router(
        0, col_window, row_windows
    )
    got = beat(0, [])
    pieces = send_columns(strips, 0)
    tables = tables_of(no_turns)
    got, pieces, chunks, tables, local_mask = fence((got, pieces, chunks, tables, local_mask))
    row_chunks = row_chunks + gather(chunks[1:])

    placed = join_columns(pieces)
    halfway = first_rows(placed, row_turns)
    got = beat(1, got)
    got, halfway = fence((got, halfway))

    near = second_rows(halfway, row_turns)
    got, near, row_chunks[2] = fence((got, near, row_chunks[2]))

    got = beat(2, got)
    far = third_rows(near, row_turns)
    base = extend(front_trailing, near, far, tables, False)
    got = beat(3, got)
    columns = [columns_of(0, got)]
    got, base, columns, row_chunks[4] = fence((got, base, columns, row_chunks[4]))

    row_rounds = [rounds_of(edges, size) for edges, size in zip(row_edges, row_windows)]
    every_round = functools.reduce(lambda a, b: a * b, row_rounds)

    def more_rows(turn, base):
        turns = turns_of(turn, row_rounds)
        near = second_rows(first_rows(placed, turns), turns)
        return extend(base, near, third_rows(near, turns), tables_of([0] + turns))

    base = lax.fori_loop(1, every_round, more_rows, base)

    most = jnp.max(col_edges[:, 1:] - col_edges[:, :-1])
    ranges = [pattern.shape[0] // count for count in (subs, subs * rows // cores, grid)]
    sends, joins, firsts, seconds, thirds, tables_at = router(
        col_window, MORE_COLUMNS, [min(size, child_tiles) for size in ranges]
    )

    def more_columns(turn, base):
        near = seconds(firsts(joins(sends(strips, turn)), row_turns), row_turns)
        return extend(base, near, thirds(near, row_turns), tables_at([turn] + row_turns))

    left = jnp.maximum(most - col_window, 0)
    base = lax.fori_loop(0, (left + MORE_COLUMNS - 1) // MORE_COLUMNS, more_columns, base)

    columns.append(columns_of(1, got))
    got = beat(4, got)
    columns.append(columns_of(2, got))
    got = beat(5, got)
    got, base, columns = fence((got, base, columns))

    base = subtract(base, 0, columns)
    straight = [hand_on(held, [(0, way[3])]) for held, way in zip(halves_of(5), ring)]
    got = beat(6, got)

    base, got, straight = fence((base, got, straight))
    columns = [columns_of(3, got), columns_of(4, got), columns_of(5, got, straight)]
    base = subtract(base, 3, columns)
    return (factor, base)


def fits_line(mesh, front_trailing, child_update, tile):
    sizes = [mesh.shape[name] for name in ("sub", "row", "col")]
    grid = sizes[0] * sizes[1]
    block_rows = front_trailing.shape[0] // grid
    block_cols = front_trailing.shape[1] // sizes[2]
    child_parts = (child_update.shape[1] // sizes[2], child_update.shape[2] // sizes[1])
    return (
        sizes == [2, 4, 4]
        and block_cols == 2 * block_rows
        and all(part % tile == 0 for part in child_parts)
        and block_rows % (4 * 2 * tile) == 0
    )


def solution(mesh):
    placed = (
        P(("sub", "row", "col"), None),
        P(),
        P(("sub", "row"), "col"),
        P("sub", "col", "row"),
        P(),
        P(),
    )

    def whole(front_panel, tile_inverse, front_trailing, child_update, child_map, pattern):
        on_line = fits_line(mesh, front_trailing, child_update, tile_inverse.shape[1])
        return jax.shard_map(
            line_device if on_line else general_device,
            mesh=mesh,
            in_specs=placed,
            out_specs=(P(("sub", "row", "col"), None), P(("sub", "row"), "col")),
            check_vma=False,
        )(front_panel, tile_inverse, front_trailing, child_update, child_map, pattern)

    return whole
```
